512 devices in a mesh: blk: 256 (over x_lo, y, z, core), rep: 2 (over x_hi).
Axes of the slice: x: 4 (x_hi: 2, x_lo: 2; x = x_hi * 2 + x_lo), y: 8, z: 8, core: 2. Of those that a mesh axis runs over, the one named last changes fastest.
Arguments:
- images: bfloat16 [2, 131072, 1152], P('rep', 'blk'), may hold values from -96 to 96
- texts: bfloat16 [2, 131072, 1152], P('rep', 'blk'), may hold values from -96 to 96
- labels: int32 [2, 131072], P('rep', 'blk'), may hold values from 0 to 131071, as said below
- log_temp: float32 [1], replicated, may hold values from 4.2 to 4.6
- bias: float32 [1], replicated, may hold values from -14 to -11
Outputs:
- grad_images: bfloat16 [2, 131072, 1152], P('rep', 'blk')
- grad_texts: bfloat16 [2, 131072, 1152], P('rep', 'blk')
- stats: float32 [3], replicated
The draws below stay inside these ranges and needn't reach their ends.
Inputs may be any that keep to these rules, and one draw needn't show every extreme that they name: labels[g, i] lies in text block (i // 512 - r) mod (256) for some r with 0 <= r < 4.
All inputs are finite; a program needn't handle non-finite values.
Results may differ from the reference program's by a relative error of at most 0.0065.
Values may be sent and summed in bfloat16 or wider, within the bound.
A program may use at most 64 MiB of HBM per device.

```python
import jax
import jax.numpy as jnp
from jax import lax

D = 1152
ROWS = 512
ROUNDS = 4
PAIRS = 131072
REPLICAS = 2


def label_rows(key):
    key = jax.random.fold_in(key, 7)
    first, second = jax.random.split(key)
    blocks = PAIRS // ROWS
    owner = jnp.broadcast_to(jnp.arange(PAIRS, dtype=jnp.int32) // ROWS, (REPLICAS, PAIRS))
    back = jax.random.randint(first, (REPLICAS, PAIRS), 0, ROUNDS, dtype=jnp.int32)
    column = jax.random.randint(second, (REPLICAS, PAIRS), 0, ROWS, dtype=jnp.int32)
    return ((owner - back) % blocks * ROWS + column).astype(jnp.int32)


def rising_strength(key, low, high):
    blocks = PAIRS // ROWS
    place = (jnp.arange(PAIRS, dtype=jnp.int32) // ROWS).astype(jnp.float32)
    ceiling = low + (high - low) * (place + 0.5) / jnp.float32(blocks)
    return jax.random.uniform(key, (REPLICAS, PAIRS), jnp.float32) * ceiling[None, :]


def rising_share(key, weak, strong):
    blocks = PAIRS // ROWS
    place = (jnp.arange(PAIRS, dtype=jnp.int32) // ROWS).astype(jnp.float32)
    jitter = jax.random.uniform(key, (REPLICAS, PAIRS), jnp.float32)
    level = (place[None, :] + jitter) / jnp.float32(blocks)
    return (weak + (strong - weak) * level)[:, :, None]


def text_units(key, low, high):
    key = jax.random.fold_in(key, 11)
    key_center, key_topic, key_strength, key_noise = jax.random.split(key, 4)
    topic_count = 64
    root_width = jnp.sqrt(jnp.float32(D))
    centers = jax.random.normal(key_center, (topic_count, D), jnp.float32) / root_width
    topic = jax.random.randint(key_topic, (REPLICAS, PAIRS), 0, topic_count, dtype=jnp.int32)
    strength = rising_strength(key_strength, low, high)
    noise = jax.random.normal(key_noise, (REPLICAS, PAIRS, D), jnp.float32) / root_width
    unit = jnp.sqrt(strength)[:, :, None] * centers[topic] + jnp.sqrt(1.0 - strength)[:, :, None] * noise
    return (unit, centers, topic)


def scaled_rows(key, unit, small, large):
    spread = jax.random.uniform(key, (REPLICAS, PAIRS, 1), jnp.float32, jnp.log(small), jnp.log(large))
    values = unit * jnp.exp(spread) * jnp.sqrt(jnp.float32(D))
    return jnp.clip(values, -96.0, 96.0).astype(jnp.bfloat16)


def draw_labels(key, part):
    return label_rows(key)


def draw_texts(key, part):
    low, high, small, large = (0.06, 0.2, 2.0, 8.0)
    unit, centers, topic = text_units(key, low, high)
    key = jax.random.fold_in(key, 17)
    return scaled_rows(key, unit, small, large)


def draw_images(key, part):
    low, high, small, large, weak, strong = (0.06, 0.2, 2.0, 8.0, 0.04, 0.4)
    unit, centers, topic = text_units(key, low, high)
    labels = label_rows(key)
    key = jax.random.fold_in(key, 13)
    key_share, key_strength, key_noise, key_scale = jax.random.split(key, 4)
    partner = jnp.take_along_axis(unit, labels[:, :, None], axis=1)
    partner_topic = jnp.take_along_axis(topic, labels, axis=1)
    strength = rising_strength(key_strength, low, high)
    noise = jax.random.normal(key_noise, (REPLICAS, PAIRS, D), jnp.float32) / jnp.sqrt(jnp.float32(D))
    own_part = jnp.sqrt(strength)[:, :, None] * centers[partner_topic] + jnp.sqrt(1.0 - strength)[:, :, None] * noise
    share = rising_share(key_share, weak, strong)
    mixed = share * partner + jnp.sqrt(1.0 - share * share) * own_part
    return scaled_rows(key_scale, mixed, small, large)


def setup_inputs(seed: int = 0) -> dict:
    seeds = jax.random.split(jax.random.key(seed), 6)
    return {
        "images": draw_images(jax.random.fold_in(seeds[5], 71), 0),
        "texts": draw_texts(jax.random.fold_in(seeds[5], 71), 0),
        "labels": draw_labels(jax.random.fold_in(seeds[5], 71), 0),
        "log_temp": jnp.clip(jax.random.uniform(seeds[3], (1,), jnp.float32, 4.2, 4.6), 4.2, 4.6),
        "bias": jnp.clip(jax.random.uniform(seeds[4], (1,), jnp.float32, -14.0, -11.0), -14.0, -11.0),
    }


EPS = 1e-06

def normalize(rows):
    rows32 = rows.astype(jnp.float32)
    rinv = lax.rsqrt(lax.optimization_barrier(jnp.sum(rows32 * rows32, axis=-1, keepdims=True)) + EPS)
    return (rows32 * rinv, rinv)

def project_back(grad, unit, rinv):
    return ((grad - unit * lax.optimization_barrier(jnp.sum(unit * grad, axis=-1, keepdims=True))) * rinv).astype(jnp.bfloat16)

def reference(images, texts, labels, log_temp, bias):
    temp = jnp.exp(log_temp[0])
    shift_b = bias[0]
    blocks = PAIRS // ROWS
    out_img = []
    out_txt = []
    loss_sum = jnp.float32(0.0)
    temp_sum = jnp.float32(0.0)
    bias_sum = jnp.float32(0.0)
    for group in range(REPLICAS):
        xn32, rinv_x = normalize(images[group])
        yn32, rinv_y = normalize(texts[group])
        xn = xn32.astype(jnp.bfloat16).reshape(blocks, ROWS, D).astype(jnp.float32)
        yn = yn32.astype(jnp.bfloat16).reshape(blocks, ROWS, D).astype(jnp.float32)
        lab = labels[group].reshape(blocks, ROWS)
        grad_x = jnp.zeros((blocks, ROWS, D), jnp.float32)
        grad_y = jnp.zeros((blocks, ROWS, D), jnp.float32)
        for offset in range(ROUNDS):
            moved = jnp.roll(yn, offset, axis=0)
            owner = ((jnp.arange(blocks, dtype=jnp.int32) - offset) % blocks).astype(jnp.int32)
            ident = owner[:, None] * ROWS + jnp.arange(ROWS, dtype=jnp.int32)[None, :]
            sign = jnp.where(lab[:, :, None] == ident[:, None, :], 1.0, -1.0).astype(jnp.float32)
            scaled = temp * jnp.einsum('kid,kjd->kij', xn, moved)
            logit = scaled + shift_b
            loss_sum = loss_sum + jnp.sum(-jax.nn.log_sigmoid(sign * logit))
            slope = -sign * jax.nn.sigmoid(-sign * logit)
            temp_sum = temp_sum + jnp.sum(slope * scaled)
            bias_sum = bias_sum + jnp.sum(slope)
            weight = (temp * slope).astype(jnp.bfloat16).astype(jnp.float32)
            grad_x = grad_x + jnp.einsum('kij,kjd->kid', weight, moved)
            grad_y = grad_y + jnp.roll(jnp.einsum('kij,kid->kjd', weight, xn), -offset, axis=0)
        out_img.append(project_back(grad_x.reshape(PAIRS, D), xn32, rinv_x))
        out_txt.append(project_back(grad_y.reshape(PAIRS, D), yn32, rinv_y))
    stats = jnp.stack([loss_sum, temp_sum, bias_sum]) / jnp.float32(REPLICAS * PAIRS)
    return (jnp.stack(out_img), jnp.stack(out_txt), stats)
```

```python
import functools

import jax
import jax.numpy as jnp
from jax import lax
from jax.experimental import pallas as pl
from jax.experimental.pallas import tpu as pltpu
from jax.sharding import PartitionSpec as P

MESH = pl.DeviceIdType.MESH
EPS = 1e-06
F32 = jnp.float32
BF16 = jnp.bfloat16
ROWS = 512
D = 1152
CH = 64
NCH = ROWS // CH
ZS, YS, XS = 8, 8, 2


def kernel(blocks, reps, images, texts, labels, log_temp, bias, o_img, o_txt, o_stats,
           buf, raw, acc, rinv, rowv, colv, consts, sbuf, st, arbuf,
           ld, ldl, zs, zr, ps, pr, f1s, f1r, f3s, f3r, fas, far_r, ls, lr,
           os_, or_, bs_, br, ars, arr, rdy, fargo):
    me = lax.axis_index("blk")
    rep = lax.axis_index("rep")
    core = lax.rem(me, 2)
    F = core
    N = 1 - core
    sgn = 2 * core - 1

    def at(step):
        return lax.rem(me + step + blocks, blocks)

    peer, far = at(-sgn), at(sgn)
    even, odd = core == 0, core == 1
    z = lax.rem(me // 2, ZS)
    y = lax.rem(me // (2 * ZS), YS)
    x = me // (2 * ZS * YS)
    xi = x * reps + rep

    def x_mate(j):
        i = lax.rem(xi + j, XS * reps)
        return {"blk": me + (i // reps - x) * (2 * ZS * YS), "rep": lax.rem(i, reps)}

    def y_mate(j):
        return {"blk": me + (lax.rem(y + j, YS) - y) * (2 * ZS)}

    def z_mate(j):
        return {"blk": me + (lax.rem(z + j, ZS) - z) * 2}

    groups = [(XS * reps, xi, x_mate), (YS, y, y_mate), (ZS, z, z_mate)]

    bar = pltpu.get_barrier_semaphore()

    def hello(step):
        pl.semaphore_signal(bar, inc=1, device_id={"blk": at(step)}, device_id_type=MESH)

    hello(2)
    hello(-2)

    @pl.when(odd)
    def _():
        for step in (1, -1, 3, -3):
            hello(step)

    @pl.when(even)
    def _():
        for size, _, mate in groups:
            for j in range(1, size):
                pl.semaphore_signal(bar, inc=1, device_id=mate(j), device_id_type=MESH)

    LB = 128
    srcs = (images, texts)

    def load(f, j):
        s = pl.ds(j * LB, LB)
        return pltpu.make_async_copy(srcs[f].at[0, s], raw.at[f, s], ld.at[f, j])

    for j in range(ROWS // LB):
        for f in (0, 1):
            load(f, j).start()
    lab_load = pltpu.make_async_copy(labels, rowv.at[1, 0], ldl)
    lab_load.start()

    def z_send(f, k):
        s = pl.ds(k * CH, CH)
        return pltpu.make_async_remote_copy(
            src_ref=buf.at[f, 0, s], dst_ref=buf.at[f, 2, s], send_sem=zs.at[f, k], recv_sem=zr.at[f, k],
            device_id={"blk": at(4 * f - 2)}, device_id_type=MESH)

    def peer_send(j):
        s = pl.ds(j * LB, LB)
        return pltpu.make_async_remote_copy(
            src_ref=buf.at[N, 0, s], dst_ref=buf.at[N, 1, s], send_sem=ps.at[j], recv_sem=pr.at[j],
            device_id={"blk": peer}, device_id_type=MESH)

    def pass_on(f, slot_to, k, ss, rs, to):
        s = pl.ds(k * CH, CH)
        return pltpu.make_async_remote_copy(
            src_ref=buf.at[f, 2, s], dst_ref=buf.at[f, slot_to, s], send_sem=ss.at[k], recv_sem=rs.at[k],
            device_id={"blk": to}, device_id_type=MESH)

    def fwd_f(k):
        return pass_on(F, 1, k, f1s, f1r, peer)

    def fwd_n(k):
        return pass_on(N, 3, k, f3s, f3r, peer)

    def far_send(k):
        return pass_on(F, 3, k, fas, far_r, far)

    for j in range(ROWS // LB):
        for f in (0, 1):
            load(f, j).wait()
            s = slice(j * LB, (j + 1) * LB)
            x32 = raw[f, s, :].astype(F32)
            r = lax.rsqrt(jnp.sum(x32 * x32, axis=-1, keepdims=True) + EPS)
            buf[f, 0, s, :] = (x32 * r).astype(BF16)
            rinv[f, s, :] = jnp.broadcast_to(r, (LB, 128))
        if j == 0:

            @pl.when(even)
            def _():
                pl.semaphore_wait(bar, 6 + sum(size - 1 for size, _, _ in groups))
                for step in (1, -1, 3, -3):
                    pl.semaphore_signal(rdy, inc=1, device_id={"blk": at(step)}, device_id_type=MESH)

            @pl.when(odd)
            def _():
                pl.semaphore_wait(bar, 2)

        for k in range(j * LB // CH, (j + 1) * LB // CH):
            for f in (0, 1):
                z_send(f, k).start()

    lab_load.wait()

    def lab_send(r):
        return pltpu.make_async_remote_copy(
            src_ref=rowv.at[1, 0], dst_ref=rowv.at[1, r], send_sem=ls.at[r - 1], recv_sem=lr.at[r - 1],
            device_id={"blk": at(-r)}, device_id_type=MESH)

    @pl.when(odd)
    def _():
        pl.semaphore_wait(rdy, 4)

    for j in range(ROWS // LB):
        peer_send(j).start()
    for r in (1, 2, 3):
        lab_send(r).start()

    lane = lax.broadcasted_iota(jnp.int32, (1, ROWS), 1)
    for r in range(4):
        rowv[0, r] = lane + at(-r) * ROWS
    colv[0] = jnp.transpose(jnp.broadcast_to(rowv[1, 0].astype(F32), (128, ROWS))).astype(jnp.int32)
    colv[1] = lax.broadcasted_iota(jnp.int32, (ROWS, 128), 0) + me * ROWS
    consts[0] = jnp.exp(jnp.full((1, 256), log_temp[0], F32))
    consts[1] = jnp.full((1, 256), bias[0], F32)
    st[...] = jnp.zeros_like(st)

    def clear(i, _):
        for f in (0, 1):
            acc[f, pl.ds(pl.multiple_of(i * 64, 64), 64), :] = jnp.zeros((64, D), F32)
        return 0

    lax.fori_loop(0, ROWS // 64, clear, 0)

    def matches(f, rb, rows, r, c0, width, shift):
        ids = colv[f, rb:rb + rows, :]
        ids = jnp.concatenate([ids] * (width // 128), axis=1) if width > 128 else ids
        return ids == rowv[f, r, :, pl.ds(c0, width)] - shift

    def item(f, own, r, c0, width, flag=None, shift=0, grad=True):
        RB = 256
        for rb in range(0, ROWS, RB):
            other = buf[1 - f, r, pl.ds(c0, width), :]
            scaled = consts[0, :, :width] * lax.dot_general(
                buf[f, own, rb:rb + RB, :], other, (((1,), (1,)), ((), ())), preferred_element_type=F32)
            if flag is not None:
                sbuf[rb:rb + RB, :width] = scaled
            if grad:
                logit = scaled + consts[1, :, :width]
                m = matches(f, rb, RB, r, c0, width, shift)
                sig = 1.0 / (1.0 + jnp.exp(jnp.where(m, logit, -logit)))
                w = (consts[0, :, :width] * jnp.where(m, -sig, sig)).astype(BF16)
                acc[f, rb:rb + RB, :] += jnp.dot(w, other, preferred_element_type=F32)
        if flag is None:
            return

        @pl.when(flag)
        def _():
            SB = 64
            tot = [jnp.zeros((8, 128), F32)] * 3
            for rb in range(0, ROWS, SB):
                scaled = sbuf[rb:rb + SB, :width]
                logit = scaled + consts[1, :, :width]
                m = matches(f, rb, SB, r, c0, width, shift)
                u = jnp.where(m, logit, -logit)
                e = jnp.exp(-jnp.abs(u))
                inv = 1.0 / (1.0 + e)
                sig = jnp.where(u >= 0, e * inv, inv)
                g = jnp.where(m, -sig, sig)
                loss = jnp.maximum(-u, 0.0) + jnp.log1p(e)
                for i, v in enumerate((loss, g * scaled, g)):
                    v = jnp.sum(v.reshape(SB // 8, 8, width), axis=0)
                    for c in range(0, width, 128):
                        tot[i] = tot[i] + v[:, c:c + 128]
            for i in range(3):
                st[i] += tot[i]

    def counted(f, r):
        return jnp.logical_and(f == 0, jnp.logical_or(odd, r < 3))

    def early(i, _):
        r = i // 4
        f = jnp.where(r == 0, i // 2, N)
        h = lax.rem(i, 2)

        @pl.when(i == 4)
        def _():
            for r_ in (1, 2, 3):
                lab_send(r_).wait_recv()
            for j in range(ROWS // LB):
                peer_send(j).wait_recv()

        item(f, 0, r, pl.multiple_of(h * 256, 256), 256, counted(f, r))
        return 0

    lax.fori_loop(0, 6, early, 0)

    def near(q, _):
        for j in (0, 1):
            k = 2 * q + j
            z_send(F, k).wait_recv()
            fwd_f(k).start()
            z_send(N, k).wait_recv()
            fwd_n(k).start()

            @pl.when(q == 3)
            def _():
                if j == 0:
                    def sent(k_, _):
                        z_send(N, k_).wait_send()
                        return 0

                    lax.fori_loop(0, 6, sent, 0)
                    pl.semaphore_signal(fargo, inc=1, device_id={"blk": peer}, device_id_type=MESH)
                    pl.semaphore_wait(fargo, 1)

                def go(k_, _):
                    far_send(k_).start()
                    return 0

                lax.fori_loop(4 * j, 4 * j + 4, go, 0)

        def sub(i, _):
            side = jnp.logical_or(i == 0, i == 3)
            f = jnp.where(side, N, F)
            r = jnp.where(i < 2, 2, jnp.where(i == 2, 1, 3))

            @pl.when(i == 2)
            def _():
                for j in (0, 1):
                    fwd_f(2 * q + j).wait_recv()
                    fwd_n(2 * q + j).wait_recv()

            item(f, 0, r, pl.multiple_of(q * 128, 128), 128, counted(f, r))
            return 0

        lax.fori_loop(0, 4, sub, 0)
        return 0

    lax.fori_loop(0, 4, near, 0)

    @pl.when(even)
    def _():
        def both(h, _):
            item(1, 1, 2, pl.multiple_of(h * 256, 256), 256, flag=h >= 0, shift=(at(-1) - me) * ROWS, grad=False)
            return 0

        lax.fori_loop(0, 2, both, 0)

    row = lax.broadcasted_iota(jnp.int32, (8, 128), 0)
    tile = jnp.zeros((8, 128), F32)
    for i in range(3):
        tile = jnp.where(row == i, jnp.broadcast_to(jnp.sum(st[i], axis=0, keepdims=True), (8, 128)), tile)

    up = pltpu.make_async_remote_copy(
        src_ref=arbuf.at[3, 2], dst_ref=arbuf.at[3, 0], send_sem=os_, recv_sem=or_, device_id={"blk": peer},
        device_id_type=MESH)
    down = pltpu.make_async_remote_copy(
        src_ref=arbuf.at[3, 2], dst_ref=arbuf.at[3, 1], send_sem=bs_, recv_sem=br, device_id={"blk": peer},
        device_id_type=MESH)

    def ar_copy(step, j, source):
        _, i, mate = groups[step]
        return pltpu.make_async_remote_copy(
            src_ref=arbuf.at[step, i], dst_ref=arbuf.at[step, i], send_sem=ars.at[step, j], recv_sem=arr.at[step, source],
            device_id=mate(j), device_id_type=MESH)

    def ar_send(step, value):
        size, i, _ = groups[step]
        arbuf[step, i] = value
        for j in range(1, size):
            ar_copy(step, j, i).start()

    def ar_sum(step):
        size, i, _ = groups[step]
        for j in range(1, size):
            ar_copy(step, j, lax.rem(i + j, size)).wait_recv()
        total = arbuf[step, 0]
        for j in range(1, size):
            total = total + arbuf[step, j]
        return total

    @pl.when(odd)
    def _():
        arbuf[3, 2] = tile
        up.start()

    def ar_step(step):
        @pl.when(even)
        def _():
            if step == 0:
                up.wait_recv()
                ar_send(0, tile + arbuf[3, 0])
            elif step < 3:
                ar_send(step, ar_sum(step - 1))
            else:
                arbuf[3, 2] = ar_sum(2)
                down.start()

    ar_step(0)

    def finish(f, out):
        FB = 64

        def rows_(i, _):
            s = pl.ds(pl.multiple_of(i * FB, FB), FB)
            d = acc[f, s, :]
            r = rinv[f, s, 0:1]
            unit = raw[f, s, :].astype(F32) * r
            dot = jnp.sum(unit * d, axis=-1, keepdims=True)
            out[0, s, :] = ((d - unit * dot) * r).astype(BF16)
            return 0

        lax.fori_loop(0, ROWS // FB, rows_, 0)

    def finish_flow(f):
        @pl.when(f == 0)
        def _():
            finish(0, o_img)

        @pl.when(f == 1)
        def _():
            finish(1, o_txt)

    finish_flow(N)

    for q in range(4):
        for k in (2 * q, 2 * q + 1):
            pltpu.make_async_remote_copy(
                src_ref=buf.at[N, 2, pl.ds(k * CH, CH)], dst_ref=buf.at[N, 3, pl.ds(k * CH, CH)], send_sem=fas.at[k],
                recv_sem=far_r.at[k], device_id={"blk": far}, device_id_type=MESH).wait_recv()
        item(F, 0, 3, q * 128, 128)
        if q < 3:
            ar_step(q + 1)

    finish_flow(F)

    @pl.when(odd)
    def _():
        down.wait_recv()

    fin = jnp.where(odd, arbuf[3, 1], arbuf[3, 2])
    for i in range(3):
        o_stats[i] = jnp.sum(fin[i:i + 1, :]) / F32(blocks * reps * ROWS)

    def left(k, _):
        z_send(F, k).wait_send()
        fwd_f(k).wait_send()
        fwd_n(k).wait_send()
        far_send(k).wait_send()
        return 0

    lax.fori_loop(0, NCH, left, 0)
    for k in (6, 7):
        z_send(N, k).wait_send()
    for j in range(ROWS // LB):
        peer_send(j).wait_send()
    for r in (1, 2, 3):
        lab_send(r).wait_send()

    @pl.when(odd)
    def _():
        up.wait_send()

    @pl.when(even)
    def _():
        for step in range(3):
            for j in range(1, groups[step][0]):
                ar_copy(step, j, 0).wait_send()
        down.wait_send()


def solution(mesh):
    blocks, reps = mesh.shape["blk"], mesh.shape["rep"]
    hbm = pl.BlockSpec(memory_space=pltpu.HBM)
    vmem = pl.BlockSpec(memory_space=pltpu.VMEM)
    smem = pl.BlockSpec(memory_space=pltpu.SMEM)
    dma = pltpu.SemaphoreType.DMA
    reg = pltpu.SemaphoreType.REGULAR

    def step(images, texts, labels, log_temp, bias):
        shape = (1, ROWS, D)
        return pl.pallas_call(
            functools.partial(kernel, blocks, reps),
            out_shape=(pltpu.VMEM(shape, BF16), pltpu.VMEM(shape, BF16), jax.ShapeDtypeStruct((3,), F32)),
            in_specs=[hbm, hbm, hbm, smem, smem],
            out_specs=(vmem, vmem, smem),
            scratch_shapes=[
                pltpu.VMEM((2, 4, ROWS, D), BF16),
                pltpu.VMEM((2, ROWS, D), BF16),
                pltpu.VMEM((2, ROWS, D), F32),
                pltpu.VMEM((2, ROWS, 128), F32),
                pltpu.VMEM((2, 4, 1, ROWS), jnp.int32),
                pltpu.VMEM((2, ROWS, 128), jnp.int32),
                pltpu.VMEM((2, 1, 256), F32),
                pltpu.VMEM((ROWS, 256), F32),
                pltpu.VMEM((3, 8, 128), F32),
                pltpu.VMEM((4, 8, 8, 128), F32),
                dma((2, 4)), dma,
                dma((2, NCH)), dma((2, NCH)), dma((4,)), dma((4,)),
                dma((NCH,)), dma((NCH,)), dma((NCH,)), dma((NCH,)), dma((NCH,)), dma((NCH,)),
                dma((3,)), dma((3,)),
                dma, dma, dma, dma, dma((3, 8)), dma((3, 8)),
                reg, reg,
            ],
            compiler_params=pltpu.CompilerParams(
                collective_id=0, has_side_effects=True, vmem_limit_bytes=48 * 2**20),
            name="siglip",
        )(images, texts, labels, log_temp, bias)

    return jax.shard_map(
        step,
        mesh=mesh,
        in_specs=(P("rep", "blk", None), P("rep", "blk", None), P("rep", "blk"), P(), P()),
        out_specs=(P("rep", "blk", None), P("rep", "blk", None), P()),
        check_vma=False,
    )
```

```python
import functools

import jax
import jax.numpy as jnp
from jax import lax
from jax.experimental import pallas as pl
from jax.experimental.pallas import tpu as pltpu
from jax.sharding import PartitionSpec as P

MESH = pl.DeviceIdType.MESH
EPS = 1e-06
F32 = jnp.float32
BF16 = jnp.bfloat16
ROWS = 512
D = 1152
CH = 64
NCH = ROWS // CH
GO_AT = 5
ZS, YS, XS = 8, 8, 2


def kernel(blocks, reps, images, texts, labels, log_temp, bias, o_img, o_txt, o_stats,
           buf, raw, acc, rinv, rowv, colv, consts, sbuf, st, arbuf,
           ld, ldl, zs, zr, ps, pr, f1s, f1r, f3s, f3r, fas, far_r, ls, lr,
           os_, or_, ars, arr, rdy, go, fargo):
    me = lax.axis_index("blk")
    rep = lax.axis_index("rep")
    core = lax.rem(me, 2)
    F = core
    N = 1 - core
    sgn = 2 * core - 1

    def at(step):
        return lax.rem(me + step + blocks, blocks)

    peer, far = at(-sgn), at(sgn)
    even, odd = core == 0, core == 1
    z = lax.rem(me // 2, ZS)
    y = lax.rem(me // (2 * ZS), YS)
    x = me // (2 * ZS * YS)
    xi = x * reps + rep

    def x_mate(j):
        i = lax.rem(xi + j, XS * reps)
        return {"blk": me + (i // reps - x) * (2 * ZS * YS), "rep": lax.rem(i, reps)}

    def y_mate(j):
        return {"blk": me + (lax.rem(y + j, YS) - y) * (2 * ZS)}

    def z_mate(j):
        return {"blk": me + (lax.rem(z + j, ZS) - z) * 2}

    def z_odd(j):
        return {"blk": me + 1 + (lax.rem(z + j, ZS) - z) * 2}

    groups = [(XS * reps, xi, x_mate), (YS, y, y_mate), (ZS, z, z_mate)]

    bar = pltpu.get_barrier_semaphore()

    def hello(step):
        pl.semaphore_signal(bar, inc=1, device_id={"blk": at(step)}, device_id_type=MESH)

    hello(2)
    hello(-2)

    @pl.when(odd)
    def _():
        for step in (1, -1, 3, -3):
            hello(step)
        for j in range(ZS):
            pl.semaphore_signal(bar, inc=1, device_id={"blk": z_mate(j)["blk"] - 1}, device_id_type=MESH)

    @pl.when(even)
    def _():
        for size, _, mate in groups:
            for j in range(1, size):
                pl.semaphore_signal(bar, inc=1, device_id=mate(j), device_id_type=MESH)

    LB = 128
    srcs = (images, texts)

    def load(f, j):
        s = pl.ds(j * LB, LB)
        return pltpu.make_async_copy(srcs[f].at[0, s], raw.at[f, s], ld.at[f, j])

    for j in range(ROWS // LB):
        for f in (0, 1):
            load(f, j).start()
    lab_load = pltpu.make_async_copy(labels, rowv.at[1, 0], ldl)
    lab_load.start()

    def z_send(f, k):
        s = pl.ds(k * CH, CH)
        return pltpu.make_async_remote_copy(
            src_ref=buf.at[f, 0, s], dst_ref=buf.at[f, 2, s], send_sem=zs.at[f, k], recv_sem=zr.at[f, k],
            device_id={"blk": at(4 * f - 2)}, device_id_type=MESH)

    def peer_send(j):
        s = pl.ds(j * LB, LB)
        return pltpu.make_async_remote_copy(
            src_ref=buf.at[N, 0, s], dst_ref=buf.at[N, 1, s], send_sem=ps.at[j], recv_sem=pr.at[j],
            device_id={"blk": peer}, device_id_type=MESH)

    def pass_on(f, slot_to, k, ss, rs, to):
        s = pl.ds(k * CH, CH)
        return pltpu.make_async_remote_copy(
            src_ref=buf.at[f, 2, s], dst_ref=buf.at[f, slot_to, s], send_sem=ss.at[k], recv_sem=rs.at[k],
            device_id={"blk": to}, device_id_type=MESH)

    def fwd_f(k):
        return pass_on(F, 1, k, f1s, f1r, peer)

    def fwd_n(k):
        return pass_on(N, 3, k, f3s, f3r, peer)

    def far_send(k):
        return pass_on(F, 3, k, fas, far_r, far)

    def far_recv(k):
        return pass_on(N, 3, k, fas, far_r, far)

    def lab_send(r):
        return pltpu.make_async_remote_copy(
            src_ref=rowv.at[1, 0], dst_ref=rowv.at[1, r], send_sem=ls.at[r - 1], recv_sem=lr.at[r - 1],
            device_id={"blk": at(-r)}, device_id_type=MESH)

    def each(lo, hi, fn):
        def step(k, _):
            fn(k)
            return 0

        lax.fori_loop(lo, hi, step, 0)

    for j in range(ROWS // LB):
        for f in (0, 1):
            load(f, j).wait()
            s = slice(j * LB, (j + 1) * LB)
            x32 = raw[f, s, :].astype(F32)
            r = lax.rsqrt(jnp.sum(x32 * x32, axis=-1, keepdims=True) + EPS)
            buf[f, 0, s, :] = (x32 * r).astype(BF16)
            rinv[f, s, :] = jnp.broadcast_to(r, (LB, 128))

        @pl.when(odd)
        def _():
            if j == 0:
                pl.semaphore_wait(bar, 2)
            for k in range(j * LB // CH, (j + 1) * LB // CH):
                for f in (0, 1):
                    z_send(f, k).start()

    lab_load.wait()
    lane = lax.broadcasted_iota(jnp.int32, (1, ROWS), 1)
    for r in range(4):
        rowv[0, r] = lane + at(-r) * ROWS
    colv[0] = jnp.transpose(jnp.broadcast_to(rowv[1, 0].astype(F32), (128, ROWS))).astype(jnp.int32)
    colv[1] = lax.broadcasted_iota(jnp.int32, (ROWS, 128), 0) + me * ROWS
    consts[0] = jnp.exp(jnp.full((1, ROWS), log_temp[0], F32))
    consts[1] = jnp.full((1, ROWS), bias[0], F32)
    st[...] = jnp.zeros_like(st)

    def clear(i):
        for f in (0, 1):
            acc[f, pl.ds(pl.multiple_of(i * 64, 64), 64), :] = jnp.zeros((64, D), F32)

    each(0, ROWS // 64, clear)

    def matches(f, rows, r, c0, width, shift=0):
        ids = colv[f, rows, :]
        ids = jnp.concatenate([ids] * (width // 128), axis=1) if width > 128 else ids
        return ids == rowv[f, r, :, pl.ds(c0, width)] - shift

    def scores(f, own, rb, rows, r, c0, width):
        return consts[0, :, :width] * lax.dot_general(
            buf[f, own, rb:rb + rows, :], buf[1 - f, r, pl.ds(c0, width), :], (((1,), (1,)), ((), ())),
            preferred_element_type=F32)

    def item(f, r, c0, width, keep=False):
        RB = 256
        for rb in range(0, ROWS, RB):
            scaled = scores(f, 0, rb, RB, r, c0, width)
            if keep:
                sbuf[rb:rb + RB, :width] = scaled
            logit = scaled + consts[1, :, :width]
            m = matches(f, slice(rb, rb + RB), r, c0, width)
            sig = 1.0 / (1.0 + jnp.exp(jnp.where(m, logit, -logit)))
            w = (consts[0, :, :width] * jnp.where(m, -sig, sig)).astype(BF16)
            acc[f, rb:rb + RB, :] += jnp.dot(w, buf[1 - f, r, pl.ds(c0, width), :], preferred_element_type=F32)

    def tally(f, r, c0, width, shift=0):
        SB = 64 if width <= 256 else 32

        def rows_(i, tot):
            s = pl.ds(pl.multiple_of(i * SB, SB), SB)
            scaled = sbuf[s, :width]
            logit = scaled + consts[1, :, :width]
            m = matches(f, s, r, c0, width, shift)
            u = jnp.where(m, logit, -logit)
            e = jnp.exp(-jnp.abs(u))
            inv = 1.0 / (1.0 + e)
            sig = jnp.where(u >= 0, e * inv, inv)
            g = jnp.where(m, -sig, sig)
            loss = jnp.maximum(-u, 0.0) + jnp.log1p(e)
            out = []
            for t, v in zip(tot, (loss, g * scaled, g)):
                v = jnp.sum(v.reshape(SB // 8, 8, width), axis=0)
                for c in range(0, width, 128):
                    t = t + v[:, c:c + 128]
                out.append(t)
            return tuple(out)

        tot = lax.fori_loop(0, ROWS // SB, rows_, tuple(jnp.zeros((8, 128), F32) for _ in range(3)))
        for i in range(3):
            st[i] += tot[i]

    def tile():
        row = lax.broadcasted_iota(jnp.int32, (8, 128), 0)
        out = jnp.zeros((8, 128), F32)
        for i in range(3):
            out = jnp.where(row == i, jnp.broadcast_to(jnp.sum(st[i], axis=0, keepdims=True), (8, 128)), out)
        return out

    up = pltpu.make_async_remote_copy(
        src_ref=arbuf.at[3, 1], dst_ref=arbuf.at[3, 0], send_sem=os_, recv_sem=or_, device_id={"blk": peer},
        device_id_type=MESH)

    def ar_copy(step, n, to, source):
        i = groups[step][1]
        return pltpu.make_async_remote_copy(
            src_ref=arbuf.at[step, i], dst_ref=arbuf.at[step, i], send_sem=ars.at[step, n],
            recv_sem=arr.at[step, source], device_id=to, device_id_type=MESH)

    def ar_sends(step):
        size, i, mate = groups[step]
        sends = [ar_copy(step, j - 1, mate(j), i) for j in range(1, size)]
        if step == 2:
            sends += [ar_copy(step, size - 1 + j, z_odd(j), i) for j in range(size)]
        return sends

    def ar_send(step, value):
        arbuf[step, groups[step][1]] = value
        for c in ar_sends(step):
            c.start()

    def ar_sum(step, first=1):
        size, i, mate = groups[step]
        for j in range(first, size):
            ar_copy(step, 0, mate(j) if j else z_odd(0), lax.rem(i + j, size)).wait_recv()
        total = arbuf[step, 0]
        for j in range(1, size):
            total = total + arbuf[step, j]
        return total

    def before_first_near():
        @pl.when(even)
        def _():
            pl.semaphore_wait(bar, 6 + ZS + sum(size - 1 for size, _, _ in groups))
            for step in (1, -1, 3, -3):
                pl.semaphore_signal(rdy, inc=1, device_id={"blk": at(step)}, device_id_type=MESH)

        @pl.when(odd)
        def _():
            pl.semaphore_wait(rdy, 4)

        for j in range(ROWS // LB):
            peer_send(j).start()
        for r in (1, 2, 3):
            lab_send(r).start()
        for j in range(ROWS // LB):
            peer_send(j).wait_recv()
        lab_send(1).wait_recv()

    def both_z(k):
        z_send(0, k).start()
        z_send(1, k).start()

    def both_sent(k):
        z_send(0, k).wait_send()
        z_send(1, k).wait_send()

    def pump(k):
        z_send(F, k).wait_recv()
        fwd_f(k).start()
        z_send(N, k).wait_recv()
        fwd_n(k).start()

    def tell_peer(sem):
        pl.semaphore_signal(sem, inc=1, device_id={"blk": peer}, device_id_type=MESH)

    def before_3():
        @pl.when(odd)
        def _():
            each(0, GO_AT, both_sent)
            tell_peer(go)
            each(0, NCH, pump)

        @pl.when(even)
        def _():
            pl.semaphore_wait(go, 1)
            each(0, NCH, both_z)
            each(0, NCH, lambda k: fwd_f(k).wait_recv())

        for r in (2, 3):
            lab_send(r).wait_recv()

    def before_4():
        @pl.when(odd)
        def _():
            arbuf[3, 1] = tile()
            up.start()

        @pl.when(even)
        def _():
            each(0, NCH, lambda k: fwd_n(k).wait_recv())

    def before_5():
        @pl.when(odd)
        def _():
            pl.semaphore_wait(fargo, 1)
            each(0, NCH, lambda k: far_send(k).start())
            each(0, NCH, lambda k: fwd_f(k).wait_recv())

        @pl.when(even)
        def _():
            def quarter(t):
                q, own = t // 2, lax.rem(t, 2)

                @pl.when(own == 0)
                def _():
                    pump(2 * q)
                    pump(2 * q + 1)

                    @pl.when(q == 1)
                    def _():
                        each(0, GO_AT, both_sent)
                        tell_peer(fargo)

                c0 = pl.multiple_of(q * 128, 128)
                for rb in range(0, ROWS, 256):
                    sbuf[rb:rb + 256, :128] = scores(1, own, rb, 256, 2, c0, 128)
                tally(1, 2, c0, 128, (at(-own) - me) * ROWS)

                @pl.when(jnp.logical_and(own == 1, q >= 1))
                def _():
                    each(jnp.where(q == 1, 0, 2 * q), 2 * q + 2, lambda k: far_send(k).start())

            each(0, 8, quarter)
            up.wait_recv()
            ar_send(0, tile() + arbuf[3, 0])

    def before_6():
        @pl.when(odd)
        def _():
            each(0, NCH, lambda k: fwd_n(k).wait_recv())

    syncs = {2: before_first_near, 3: before_3, 4: before_4, 5: before_5, 6: before_6}

    def pair(i):
        for at_i, sync in syncs.items():
            pl.when(i == at_i)(sync)
        via_peer = jnp.logical_or(jnp.logical_and(i < 5, even), jnp.logical_and(i >= 5, odd))
        second = lax.rem(i, 2) == 0
        late_f = jnp.where(jnp.logical_xor(via_peer, second), F, N)
        f = jnp.where(i == 1, F, jnp.where(i < 3, N, late_f))
        r = jnp.where(i < 2, 0, jnp.where(i == 2, 1, jnp.where(via_peer, jnp.where(second, 3, 1), 2)))
        item(f, r, 0, ROWS, True)
        counted = jnp.where(even, jnp.where(f == 0, r <= 1, r == 3), jnp.logical_and(f == 0, r <= 2))

        @pl.when(counted)
        def _():
            tally(f, r, 0, ROWS)

    each(0, 7, pair)

    def finish(f, out):
        FB = 64

        def rows_(i):
            s = pl.ds(pl.multiple_of(i * FB, FB), FB)
            d = acc[f, s, :]
            r = rinv[f, s, 0:1]
            unit = raw[f, s, :].astype(F32) * r
            dot = jnp.sum(unit * d, axis=-1, keepdims=True)
            out[0, s, :] = ((d - unit * dot) * r).astype(BF16)

        each(0, ROWS // FB, rows_)

    def finish_flow(f):
        @pl.when(f == 0)
        def _():
            finish(0, o_img)

        @pl.when(f == 1)
        def _():
            finish(1, o_txt)

    @pl.when(even)
    def _():
        ar_send(1, ar_sum(0))

    each(0, 4, lambda k: far_recv(k).wait_recv())
    item(F, 3, 0, 256)
    finish_flow(N)

    def last(q):
        for j in (0, 1):
            far_recv(2 * q + j).wait_recv()
        item(F, 3, pl.multiple_of(q * 128, 128), 128)

        @pl.when(jnp.logical_and(even, q == 2))
        def _():
            ar_send(2, ar_sum(1))

    each(2, 4, last)
    finish_flow(F)

    @pl.when(odd)
    def _():
        ar_sum(2, 0)

    @pl.when(even)
    def _():
        ar_sum(2)

    fin = arbuf[2, 0]
    for j in range(1, ZS):
        fin = fin + arbuf[2, j]
    for i in range(3):
        o_stats[i] = jnp.sum(fin[i:i + 1, :]) / F32(blocks * reps * ROWS)

    each(GO_AT, NCH, both_sent)

    def left(k):
        fwd_f(k).wait_send()
        fwd_n(k).wait_send()
        far_send(k).wait_send()

    each(0, NCH, left)
    for j in range(ROWS // LB):
        peer_send(j).wait_send()
    for r in (1, 2, 3):
        lab_send(r).wait_send()

    @pl.when(odd)
    def _():
        up.wait_send()

    @pl.when(even)
    def _():
        for step in range(3):
            for c in ar_sends(step):
                c.wait_send()


def solution(mesh):
    blocks, reps = mesh.shape["blk"], mesh.shape["rep"]
    hbm = pl.BlockSpec(memory_space=pltpu.HBM)
    vmem = pl.BlockSpec(memory_space=pltpu.VMEM)
    smem = pl.BlockSpec(memory_space=pltpu.SMEM)
    dma = pltpu.SemaphoreType.DMA
    reg = pltpu.SemaphoreType.REGULAR

    def step(images, texts, labels, log_temp, bias):
        shape = (1, ROWS, D)
        return pl.pallas_call(
            functools.partial(kernel, blocks, reps),
            out_shape=(pltpu.VMEM(shape, BF16), pltpu.VMEM(shape, BF16), jax.ShapeDtypeStruct((3,), F32)),
            in_specs=[hbm, hbm, hbm, smem, smem],
            out_specs=(vmem, vmem, smem),
            scratch_shapes=[
                pltpu.VMEM((2, 4, ROWS, D), BF16),
                pltpu.VMEM((2, ROWS, D), BF16),
                pltpu.VMEM((2, ROWS, D), F32),
                pltpu.VMEM((2, ROWS, 128), F32),
                pltpu.VMEM((2, 4, 1, ROWS), jnp.int32),
                pltpu.VMEM((2, ROWS, 128), jnp.int32),
                pltpu.VMEM((2, 1, ROWS), F32),
                pltpu.VMEM((ROWS, ROWS), F32),
                pltpu.VMEM((3, 8, 128), F32),
                pltpu.VMEM((4, 8, 8, 128), F32),
                dma((2, 4)), dma,
                dma((2, NCH)), dma((2, NCH)), dma((4,)), dma((4,)),
                dma((NCH,)), dma((NCH,)), dma((NCH,)), dma((NCH,)), dma((NCH,)), dma((NCH,)),
                dma((3,)), dma((3,)),
                dma, dma, dma((3, 16)), dma((3, 8)),
                reg, reg, reg,
            ],
            compiler_params=pltpu.CompilerParams(
                collective_id=0, has_side_effects=True, vmem_limit_bytes=48 * 2**20),
            name="siglip",
        )(*[pltpu.with_memory_space_constraint(v, pltpu.HBM) for v in (images, texts, labels)], log_temp, bias)

    return jax.shard_map(
        step,
        mesh=mesh,
        in_specs=(P("rep", "blk", None), P("rep", "blk", None), P("rep", "blk"), P(), P()),
        out_specs=(P("rep", "blk", None), P("rep", "blk", None), P()),
        check_vma=False,
    )
```

```python
import functools

import jax
import jax.numpy as jnp
from jax import lax
from jax.experimental import pallas as pl
from jax.experimental.pallas import tpu as pltpu
from jax.sharding import PartitionSpec as P

MESH = pl.DeviceIdType.MESH
EPS = 1e-06
F32 = jnp.float32
BF16 = jnp.bfloat16
ROWS = 512
D = 1152
CH = 64
NCH = ROWS // CH
GO_AT = 5
ZS, YS, XS = 8, 8, 2


def kernel(blocks, reps, images, texts, labels, log_temp, bias, o_img, o_txt, o_stats,
           buf, raw, acc, rinv, rowv, colv, consts, sbuf, st, arbuf,
           ld, ldl, zs, zr, ps, pr, f1s, f1r, f3s, f3r, fas, far_r, ls, lr,
           os_, or_, ars, arr, rdy, go, fargo):
    me = lax.axis_index("blk")
    rep = lax.axis_index("rep")
    core = lax.rem(me, 2)
    F = core
    N = 1 - core
    sgn = 2 * core - 1

    def at(step):
        return lax.rem(me + step + blocks, blocks)

    peer, far = at(-sgn), at(sgn)
    even, odd = core == 0, core == 1
    z = lax.rem(me // 2, ZS)
    y = lax.rem(me // (2 * ZS), YS)
    x = me // (2 * ZS * YS)
    xi = x * reps + rep

    def x_mate(j):
        i = lax.rem(xi + j, XS * reps)
        return {"blk": me + (i // reps - x) * (2 * ZS * YS), "rep": lax.rem(i, reps)}

    def y_mate(j):
        return {"blk": me + (lax.rem(y + j, YS) - y) * (2 * ZS)}

    def z_mate(j):
        return {"blk": me + (lax.rem(z + j, ZS) - z) * 2}

    def z_odd(j):
        return {"blk": me + 1 + (lax.rem(z + j, ZS) - z) * 2}

    groups = [(XS * reps, xi, x_mate), (YS, y, y_mate), (ZS, z, z_mate)]

    LB = 128
    srcs = (images, texts)

    def load(f, j):
        s = pl.ds(j * LB, LB)
        return pltpu.make_async_copy(srcs[f].at[0, s], raw.at[f, s], ld.at[f, j])

    for j in range(ROWS // LB):
        for f in (0, 1):
            load(f, j).start()
    lab_load = pltpu.make_async_copy(labels, rowv.at[1, 0], ldl)
    lab_load.start()

    bar = pltpu.get_barrier_semaphore()

    def hello(step):
        pl.semaphore_signal(bar, inc=1, device_id={"blk": at(step)}, device_id_type=MESH)

    hello(2)
    hello(-2)

    def z_send(f, k):
        s = pl.ds(k * CH, CH)
        return pltpu.make_async_remote_copy(
            src_ref=buf.at[f, 0, s], dst_ref=buf.at[f, 2, s], send_sem=zs.at[f, k], recv_sem=zr.at[f, k],
            device_id={"blk": at(4 * f - 2)}, device_id_type=MESH)

    def peer_send(j):
        s = pl.ds(j * LB, LB)
        return pltpu.make_async_remote_copy(
            src_ref=buf.at[N, 0, s], dst_ref=buf.at[N, 1, s], send_sem=ps.at[j], recv_sem=pr.at[j],
            device_id={"blk": peer}, device_id_type=MESH)

    def pass_on(f, slot_to, k, ss, rs, to):
        s = pl.ds(k * CH, CH)
        return pltpu.make_async_remote_copy(
            src_ref=buf.at[f, 2, s], dst_ref=buf.at[f, slot_to, s], send_sem=ss.at[k], recv_sem=rs.at[k],
            device_id={"blk": to}, device_id_type=MESH)

    def fwd_f(k):
        return pass_on(F, 1, k, f1s, f1r, peer)

    def fwd_n(k):
        return pass_on(N, 3, k, f3s, f3r, peer)

    def far_send(k):
        return pass_on(F, 3, k, fas, far_r, far)

    def far_recv(k):
        return pass_on(N, 3, k, fas, far_r, far)

    def lab_send(r):
        return pltpu.make_async_remote_copy(
            src_ref=rowv.at[1, 0], dst_ref=rowv.at[1, r], send_sem=ls.at[r - 1], recv_sem=lr.at[r - 1],
            device_id={"blk": at(-r)}, device_id_type=MESH)

    def each(lo, hi, fn):
        def step(k, _):
            fn(k)
            return 0

        lax.fori_loop(lo, hi, step, 0)

    for j in range(ROWS // LB):
        for f in (0, 1):
            load(f, j).wait()
            s = slice(j * LB, (j + 1) * LB)
            x32 = raw[f, s, :].astype(F32)
            r = lax.rsqrt(jnp.sum(x32 * x32, axis=-1, keepdims=True) + EPS)
            buf[f, 0, s, :] = (x32 * r).astype(BF16)
            rinv[f, s, :] = jnp.broadcast_to(r, (LB, 128))

        @pl.when(odd)
        def _():
            if j == 0:
                pl.semaphore_wait(bar, 2)
            for k in range(j * LB // CH, (j + 1) * LB // CH):
                for f in (0, 1):
                    z_send(f, k).start()

    @pl.when(odd)
    def _():
        for step in (1, -1, 3, -3):
            hello(step)
        for j in range(ZS):
            pl.semaphore_signal(bar, inc=1, device_id={"blk": z_mate(j)["blk"] - 1}, device_id_type=MESH)

    @pl.when(even)
    def _():
        for size, _, mate in groups:
            for j in range(1, size):
                pl.semaphore_signal(bar, inc=1, device_id=mate(j), device_id_type=MESH)

    lab_load.wait()
    lane = lax.broadcasted_iota(jnp.int32, (1, ROWS), 1)
    for r in range(4):
        rowv[0, r] = lane + at(-r) * ROWS
    colv[0] = jnp.transpose(jnp.broadcast_to(rowv[1, 0].astype(F32), (128, ROWS))).astype(jnp.int32)
    colv[1] = lax.broadcasted_iota(jnp.int32, (ROWS, 128), 0) + me * ROWS
    consts[0] = jnp.exp(jnp.full((1, ROWS), log_temp[0], F32))
    consts[1] = jnp.full((1, ROWS), bias[0], F32)
    st[...] = jnp.zeros_like(st)

    def clear(i):
        for f in (0, 1):
            acc[f, pl.ds(pl.multiple_of(i * 64, 64), 64), :] = jnp.zeros((64, D), F32)

    each(0, ROWS // 64, clear)

    def matches(f, rows, r, c0, width, shift=0):
        ids = colv[f, rows, :]
        ids = jnp.concatenate([ids] * (width // 128), axis=1) if width > 128 else ids
        return ids == rowv[f, r, :, pl.ds(c0, width)] - shift

    def scores(f, own, rb, rows, r, c0, width):
        return consts[0, :, :width] * lax.dot_general(
            buf[f, own, rb:rb + rows, :], buf[1 - f, r, pl.ds(c0, width), :], (((1,), (1,)), ((), ())),
            preferred_element_type=F32)

    def item(f, r, c0, width, keep=False):
        RB = 256
        for rb in range(0, ROWS, RB):
            scaled = scores(f, 0, rb, RB, r, c0, width)
            if keep:
                sbuf[rb:rb + RB, :width] = scaled
            logit = scaled + consts[1, :, :width]
            m = matches(f, slice(rb, rb + RB), r, c0, width)
            sig = 1.0 / (1.0 + jnp.exp(jnp.where(m, logit, -logit)))
            w = (consts[0, :, :width] * jnp.where(m, -sig, sig)).astype(BF16)
            acc[f, rb:rb + RB, :] += jnp.dot(w, buf[1 - f, r, pl.ds(c0, width), :], preferred_element_type=F32)

    def tally(f, r, c0, width, shift=0):
        SB = 64 if width <= 256 else 32

        def rows_(i, tot):
            s = pl.ds(pl.multiple_of(i * SB, SB), SB)
            scaled = sbuf[s, :width]
            logit = scaled + consts[1, :, :width]
            m = matches(f, s, r, c0, width, shift)
            u = jnp.where(m, logit, -logit)
            e = jnp.exp(-jnp.abs(u))
            inv = 1.0 / (1.0 + e)
            sig = jnp.where(u >= 0, e * inv, inv)
            g = jnp.where(m, -sig, sig)
            loss = jnp.maximum(-u, 0.0) + jnp.log1p(e)
            out = []
            for t, v in zip(tot, (loss, g * scaled, g)):
                v = jnp.sum(v.reshape(SB // 8, 8, width), axis=0)
                for c in range(0, width, 128):
                    t = t + v[:, c:c + 128]
                out.append(t)
            return tuple(out)

        tot = lax.fori_loop(0, ROWS // SB, rows_, tuple(jnp.zeros((8, 128), F32) for _ in range(3)))
        for i in range(3):
            st[i] += tot[i]

    def tile():
        row = lax.broadcasted_iota(jnp.int32, (8, 128), 0)
        out = jnp.zeros((8, 128), F32)
        for i in range(3):
            out = jnp.where(row == i, jnp.broadcast_to(jnp.sum(st[i], axis=0, keepdims=True), (8, 128)), out)
        return out

    up = pltpu.make_async_remote_copy(
        src_ref=arbuf.at[3, 1], dst_ref=arbuf.at[3, 0], send_sem=os_, recv_sem=or_, device_id={"blk": peer},
        device_id_type=MESH)

    def ar_copy(step, n, to, source):
        i = groups[step][1]
        return pltpu.make_async_remote_copy(
            src_ref=arbuf.at[step, i], dst_ref=arbuf.at[step, i], send_sem=ars.at[step, n],
            recv_sem=arr.at[step, source], device_id=to, device_id_type=MESH)

    def ar_sends(step):
        size, i, mate = groups[step]
        sends = [ar_copy(step, j - 1, mate(j), i) for j in range(1, size)]
        if step == 2:
            sends += [ar_copy(step, size - 1 + j, z_odd(j), i) for j in range(size)]
        return sends

    def ar_send(step, value):
        arbuf[step, groups[step][1]] = value
        for c in ar_sends(step):
            c.start()

    def ar_sum(step, first=1):
        size, i, mate = groups[step]
        for j in range(first, size):
            ar_copy(step, 0, mate(j) if j else z_odd(0), lax.rem(i + j, size)).wait_recv()
        total = arbuf[step, 0]
        for j in range(1, size):
            total = total + arbuf[step, j]
        return total

    def before_first_near():
        @pl.when(even)
        def _():
            pl.semaphore_wait(bar, 6 + ZS + sum(size - 1 for size, _, _ in groups))
            for step in (1, -1, 3, -3):
                pl.semaphore_signal(rdy, inc=1, device_id={"blk": at(step)}, device_id_type=MESH)

        @pl.when(odd)
        def _():
            pl.semaphore_wait(rdy, 4)

        for j in range(ROWS // LB):
            peer_send(j).start()
        for r in (1, 2, 3):
            lab_send(r).start()
        for j in range(ROWS // LB):
            peer_send(j).wait_recv()
        lab_send(1).wait_recv()

    def both_z(k):
        z_send(0, k).start()
        z_send(1, k).start()

    def both_sent(k):
        z_send(0, k).wait_send()
        z_send(1, k).wait_send()

    def pump(k):
        z_send(F, k).wait_recv()
        fwd_f(k).start()
        z_send(N, k).wait_recv()
        fwd_n(k).start()

    def tell_peer(sem):
        pl.semaphore_signal(sem, inc=1, device_id={"blk": peer}, device_id_type=MESH)

    def before_3():
        @pl.when(odd)
        def _():
            each(0, GO_AT, both_sent)
            tell_peer(go)
            each(0, NCH, pump)

        @pl.when(even)
        def _():
            pl.semaphore_wait(go, 1)
            each(0, NCH, both_z)
            each(0, NCH, lambda k: fwd_f(k).wait_recv())

        for r in (2, 3):
            lab_send(r).wait_recv()

    def before_4():
        @pl.when(odd)
        def _():
            arbuf[3, 1] = tile()
            up.start()

        @pl.when(even)
        def _():
            each(0, NCH, lambda k: fwd_n(k).wait_recv())

    def before_5():
        @pl.when(odd)
        def _():
            pl.semaphore_wait(fargo, 1)
            each(0, NCH, lambda k: far_send(k).start())
            each(0, NCH, lambda k: fwd_f(k).wait_recv())

        @pl.when(even)
        def _():
            def quarter(t):
                q, own = t // 2, lax.rem(t, 2)

                @pl.when(own == 0)
                def _():
                    pump(2 * q)
                    pump(2 * q + 1)

                    @pl.when(q == 1)
                    def _():
                        each(0, GO_AT, both_sent)
                        tell_peer(fargo)

                c0 = pl.multiple_of(q * 128, 128)
                for rb in range(0, ROWS, 256):
                    sbuf[rb:rb + 256, :128] = scores(1, own, rb, 256, 2, c0, 128)
                tally(1, 2, c0, 128, (at(-own) - me) * ROWS)

                @pl.when(jnp.logical_and(own == 1, q >= 1))
                def _():
                    each(jnp.where(q == 1, 0, 2 * q), 2 * q + 2, lambda k: far_send(k).start())

            each(0, 8, quarter)
            up.wait_recv()
            ar_send(0, tile() + arbuf[3, 0])

    def before_6():
        @pl.when(odd)
        def _():
            each(0, NCH, lambda k: fwd_n(k).wait_recv())

    syncs = {2: before_first_near, 3: before_3, 4: before_4, 5: before_5, 6: before_6}

    def pair(i):
        for at_i, sync in syncs.items():
            pl.when(i == at_i)(sync)
        via_peer = jnp.logical_or(jnp.logical_and(i < 5, even), jnp.logical_and(i >= 5, odd))
        second = lax.rem(i, 2) == 0
        late_f = jnp.where(jnp.logical_xor(via_peer, second), F, N)
        f = jnp.where(i == 1, F, jnp.where(i < 3, N, late_f))
        r = jnp.where(i < 2, 0, jnp.where(i == 2, 1, jnp.where(via_peer, jnp.where(second, 3, 1), 2)))
        item(f, r, 0, ROWS, True)
        counted = jnp.where(even, jnp.where(f == 0, r <= 1, r == 3), jnp.logical_and(f == 0, r <= 2))

        @pl.when(counted)
        def _():
            tally(f, r, 0, ROWS)

    each(0, 7, pair)

    def finish(f, out):
        FB = 64

        def rows_(i):
            s = pl.ds(pl.multiple_of(i * FB, FB), FB)
            d = acc[f, s, :]
            r = rinv[f, s, 0:1]
            unit = raw[f, s, :].astype(F32) * r
            dot = jnp.sum(unit * d, axis=-1, keepdims=True)
            out[0, s, :] = ((d - unit * dot) * r).astype(BF16)

        each(0, ROWS // FB, rows_)

    def finish_flow(f):
        @pl.when(f == 0)
        def _():
            finish(0, o_img)

        @pl.when(f == 1)
        def _():
            finish(1, o_txt)

    @pl.when(even)
    def _():
        ar_send(1, ar_sum(0))

    each(0, 4, lambda k: far_recv(k).wait_recv())
    item(F, 3, 0, 256)
    finish_flow(N)

    def last(q):
        for j in (0, 1):
            far_recv(2 * q + j).wait_recv()
        item(F, 3, pl.multiple_of(q * 128, 128), 128)

        @pl.when(jnp.logical_and(even, q == 2))
        def _():
            ar_send(2, ar_sum(1))

    each(2, 4, last)
    finish_flow(F)

    @pl.when(odd)
    def _():
        ar_sum(2, 0)

    @pl.when(even)
    def _():
        ar_sum(2)

    fin = arbuf[2, 0]
    for j in range(1, ZS):
        fin = fin + arbuf[2, j]
    for i in range(3):
        o_stats[i] = jnp.sum(fin[i:i + 1, :]) / F32(blocks * reps * ROWS)

    each(GO_AT, NCH, both_sent)

    def left(k):
        fwd_f(k).wait_send()
        fwd_n(k).wait_send()
        far_send(k).wait_send()

    each(0, NCH, left)
    for j in range(ROWS // LB):
        peer_send(j).wait_send()
    for r in (1, 2, 3):
        lab_send(r).wait_send()

    @pl.when(odd)
    def _():
        up.wait_send()

    @pl.when(even)
    def _():
        for step in range(3):
            for c in ar_sends(step):
                c.wait_send()


def write_out(a, b, out_a, out_b, sems):
    copies = [pltpu.make_async_copy(v, o, sems.at[i]) for i, (v, o) in enumerate(((a, out_a), (b, out_b)))]
    for copy in copies:
        copy.start()
    for copy in copies:
        copy.wait()


def solution(mesh):
    blocks, reps = mesh.shape["blk"], mesh.shape["rep"]
    hbm = pl.BlockSpec(memory_space=pltpu.HBM)
    vmem = pl.BlockSpec(memory_space=pltpu.VMEM)
    smem = pl.BlockSpec(memory_space=pltpu.SMEM)
    dma = pltpu.SemaphoreType.DMA
    reg = pltpu.SemaphoreType.REGULAR

    def step(images, texts, labels, log_temp, bias):
        shape = (1, ROWS, D)
        *grads, stats = pl.pallas_call(
            functools.partial(kernel, blocks, reps),
            out_shape=(pltpu.VMEM(shape, BF16), pltpu.VMEM(shape, BF16), jax.ShapeDtypeStruct((3,), F32)),
            in_specs=[hbm, hbm, hbm, smem, smem],
            out_specs=(vmem, vmem, smem),
            scratch_shapes=[
                pltpu.VMEM((2, 4, ROWS, D), BF16),
                pltpu.VMEM((2, ROWS, D), BF16),
                pltpu.VMEM((2, ROWS, D), F32),
                pltpu.VMEM((2, ROWS, 128), F32),
                pltpu.VMEM((2, 4, 1, ROWS), jnp.int32),
                pltpu.VMEM((2, ROWS, 128), jnp.int32),
                pltpu.VMEM((2, 1, ROWS), F32),
                pltpu.VMEM((ROWS, ROWS), F32),
                pltpu.VMEM((3, 8, 128), F32),
                pltpu.VMEM((4, 8, 8, 128), F32),
                dma((2, 4)), dma,
                dma((2, NCH)), dma((2, NCH)), dma((4,)), dma((4,)),
                dma((NCH,)), dma((NCH,)), dma((NCH,)), dma((NCH,)), dma((NCH,)), dma((NCH,)),
                dma((3,)), dma((3,)),
                dma, dma, dma((3, 16)), dma((3, 8)),
                reg, reg, reg,
            ],
            compiler_params=pltpu.CompilerParams(
                collective_id=0, has_side_effects=True, vmem_limit_bytes=48 * 2**20),
            name="siglip",
        )(*[pltpu.with_memory_space_constraint(v, pltpu.HBM) for v in (images, texts, labels)], log_temp, bias)

        full = jax.ShapeDtypeStruct(shape, BF16)
        anywhere = pl.BlockSpec(memory_space=pl.ANY)
        written = pl.pallas_call(
            write_out,
            out_shape=(full, full),
            in_specs=[anywhere] * 2,
            out_specs=(hbm, hbm),
            scratch_shapes=[dma((2,))],
            name="write_out",
        )(*[pltpu.with_memory_space_constraint(v, pltpu.VMEM) for v in grads])
        return *written, stats

    return jax.shard_map(
        step,
        mesh=mesh,
        in_specs=(P("rep", "blk", None), P("rep", "blk", None), P("rep", "blk"), P(), P()),
        out_specs=(P("rep", "blk", None), P("rep", "blk", None), P()),
        check_vma=False,
    )
```

```python
import functools

import jax
import jax.numpy as jnp
from jax import lax
from jax.experimental import pallas as pl
from jax.experimental.pallas import tpu as pltpu
from jax.sharding import PartitionSpec as P

MESH = pl.DeviceIdType.MESH
EPS = 1e-06
F32 = jnp.float32
BF16 = jnp.bfloat16
ROWS = 512
D = 1152
CH = 64
NCH = ROWS // CH
GO_AT = 5
ZS, YS, XS = 8, 8, 2


def kernel(blocks, reps, images, texts, labels, log_temp, bias, o_img, o_txt, o_stats,
           buf, raw, acc, rinv, rowv, colv, consts, sbuf, st, arbuf,
           ld, ldl, zs, zr, ps, pr, f1s, f1r, f3s, f3r, fas, far_r, ls, lr,
           os_, or_, ars, arr, rdy, go, fargo):
    me = lax.axis_index("blk")
    rep = lax.axis_index("rep")
    core = lax.rem(me, 2)
    F = core
    N = 1 - core
    sgn = 2 * core - 1

    def at(step):
        return lax.rem(me + step + blocks, blocks)

    peer, far = at(-sgn), at(sgn)
    even, odd = core == 0, core == 1
    z = lax.rem(me // 2, ZS)
    y = lax.rem(me // (2 * ZS), YS)
    x = me // (2 * ZS * YS)
    xi = x * reps + rep

    def x_mate(j):
        i = lax.rem(xi + j, XS * reps)
        return {"blk": me + (i // reps - x) * (2 * ZS * YS), "rep": lax.rem(i, reps)}

    def y_mate(j):
        return {"blk": me + (lax.rem(y + j, YS) - y) * (2 * ZS)}

    def z_mate(j):
        return {"blk": me + (lax.rem(z + j, ZS) - z) * 2}

    def z_odd(j):
        return {"blk": me + 1 + (lax.rem(z + j, ZS) - z) * 2}

    groups = [(XS * reps, xi, x_mate), (YS, y, y_mate), (ZS, z, z_mate)]

    LB = 128
    srcs = (images, texts)

    def load(f, j):
        s = pl.ds(j * LB, LB)
        return pltpu.make_async_copy(srcs[f].at[0, s], raw.at[f, s], ld.at[f, j])

    for j in range(ROWS // LB):
        for f in (0, 1):
            load(f, j).start()
    lab_load = pltpu.make_async_copy(labels, rowv.at[1, 0], ldl)
    lab_load.start()

    bar = pltpu.get_barrier_semaphore()

    def hello(step):
        pl.semaphore_signal(bar, inc=1, device_id={"blk": at(step)}, device_id_type=MESH)

    hello(2)
    hello(-2)

    def z_send(f, k):
        s = pl.ds(k * CH, CH)
        return pltpu.make_async_remote_copy(
            src_ref=buf.at[f, 0, s], dst_ref=buf.at[f, 2, s], send_sem=zs.at[f, k], recv_sem=zr.at[f, k],
            device_id={"blk": at(4 * f - 2)}, device_id_type=MESH)

    def peer_send(j):
        s = pl.ds(j * LB, LB)
        return pltpu.make_async_remote_copy(
            src_ref=buf.at[N, 0, s], dst_ref=buf.at[N, 1, s], send_sem=ps.at[j], recv_sem=pr.at[j],
            device_id={"blk": peer}, device_id_type=MESH)

    def pass_on(f, slot_to, k, ss, rs, to):
        s = pl.ds(k * CH, CH)
        return pltpu.make_async_remote_copy(
            src_ref=buf.at[f, 2, s], dst_ref=buf.at[f, slot_to, s], send_sem=ss.at[k], recv_sem=rs.at[k],
            device_id={"blk": to}, device_id_type=MESH)

    def fwd_f(k):
        return pass_on(F, 1, k, f1s, f1r, peer)

    def fwd_n(k):
        return pass_on(N, 3, k, f3s, f3r, peer)

    def far_send(k):
        return pass_on(F, 3, k, fas, far_r, far)

    def far_recv(k):
        return pass_on(N, 3, k, fas, far_r, far)

    def lab_send(r):
        return pltpu.make_async_remote_copy(
            src_ref=rowv.at[1, 0], dst_ref=rowv.at[1, r], send_sem=ls.at[r - 1], recv_sem=lr.at[r - 1],
            device_id={"blk": at(-r)}, device_id_type=MESH)

    def each(lo, hi, fn):
        def step(k, _):
            fn(k)
            return 0

        lax.fori_loop(lo, hi, step, 0)

    for j in range(ROWS // LB):
        for f in (0, 1):
            load(f, j).wait()
            s = slice(j * LB, (j + 1) * LB)
            x32 = raw[f, s, :].astype(F32)
            r = lax.rsqrt(jnp.sum(x32 * x32, axis=-1, keepdims=True) + EPS)
            buf[f, 0, s, :] = (x32 * r).astype(BF16)
            rinv[f, s, :] = jnp.broadcast_to(r, (LB, 128))

        @pl.when(odd)
        def _():
            if j == 0:
                pl.semaphore_wait(bar, 2)
            for k in range(j * LB // CH, (j + 1) * LB // CH):
                for f in (0, 1):
                    z_send(f, k).start()

    @pl.when(odd)
    def _():
        for step in (1, -1, 3, -3):
            hello(step)
        for j in range(ZS):
            pl.semaphore_signal(bar, inc=1, device_id={"blk": z_mate(j)["blk"] - 1}, device_id_type=MESH)

    @pl.when(even)
    def _():
        for size, _, mate in groups:
            for j in range(1, size):
                pl.semaphore_signal(bar, inc=1, device_id=mate(j), device_id_type=MESH)

    lab_load.wait()
    lane = lax.broadcasted_iota(jnp.int32, (1, ROWS), 1)
    for r in range(4):
        rowv[0, r] = lane + at(-r) * ROWS
    colv[0] = jnp.transpose(jnp.broadcast_to(rowv[1, 0].astype(F32), (128, ROWS))).astype(jnp.int32)
    colv[1] = lax.broadcasted_iota(jnp.int32, (ROWS, 128), 0) + me * ROWS
    consts[0] = jnp.exp(jnp.full((1, ROWS), log_temp[0], F32))
    consts[1] = jnp.full((1, ROWS), bias[0], F32)
    st[...] = jnp.zeros_like(st)

    def clear(i):
        for f in (0, 1):
            acc[f, pl.ds(pl.multiple_of(i * 64, 64), 64), :] = jnp.zeros((64, D), F32)

    each(0, ROWS // 64, clear)

    def matches(f, rows, r, c0, width, shift=0):
        ids = colv[f, rows, :]
        ids = jnp.concatenate([ids] * (width // 128), axis=1) if width > 128 else ids
        return ids == rowv[f, r, :, pl.ds(c0, width)] - shift

    def scores(f, own, rb, rows, r, c0, width):
        return consts[0, :, :width] * lax.dot_general(
            buf[f, own, rb:rb + rows, :], buf[1 - f, r, pl.ds(c0, width), :], (((1,), (1,)), ((), ())),
            preferred_element_type=F32)

    def item(f, r, c0, width, keep=False):
        RB = 256
        for rb in range(0, ROWS, RB):
            scaled = scores(f, 0, rb, RB, r, c0, width)
            if keep:
                sbuf[rb:rb + RB, :width] = scaled
            logit = scaled + consts[1, :, :width]
            m = matches(f, slice(rb, rb + RB), r, c0, width)
            sig = 1.0 / (1.0 + jnp.exp(jnp.where(m, logit, -logit)))
            w = (consts[0, :, :width] * jnp.where(m, -sig, sig)).astype(BF16)
            acc[f, rb:rb + RB, :] += jnp.dot(w, buf[1 - f, r, pl.ds(c0, width), :], preferred_element_type=F32)

    def tally(f, r, c0, width, shift=0):
        SB = 64 if width <= 256 else 32

        def rows_(i, tot):
            s = pl.ds(pl.multiple_of(i * SB, SB), SB)
            scaled = sbuf[s, :width]
            logit = scaled + consts[1, :, :width]
            m = matches(f, s, r, c0, width, shift)
            u = jnp.where(m, logit, -logit)
            e = jnp.exp(-jnp.abs(u))
            inv = 1.0 / (1.0 + e)
            sig = jnp.where(u >= 0, e * inv, inv)
            g = jnp.where(m, -sig, sig)
            loss = jnp.maximum(-u, 0.0) + jnp.log1p(e)
            out = []
            for t, v in zip(tot, (loss, g * scaled, g)):
                v = jnp.sum(v.reshape(SB // 8, 8, width), axis=0)
                for c in range(0, width, 128):
                    t = t + v[:, c:c + 128]
                out.append(t)
            return tuple(out)

        tot = lax.fori_loop(0, ROWS // SB, rows_, tuple(jnp.zeros((8, 128), F32) for _ in range(3)))
        for i in range(3):
            st[i] += tot[i]

    def tile():
        row = lax.broadcasted_iota(jnp.int32, (8, 128), 0)
        out = jnp.zeros((8, 128), F32)
        for i in range(3):
            out = jnp.where(row == i, jnp.broadcast_to(jnp.sum(st[i], axis=0, keepdims=True), (8, 128)), out)
        return out

    up = pltpu.make_async_remote_copy(
        src_ref=arbuf.at[3, 1], dst_ref=arbuf.at[3, 0], send_sem=os_, recv_sem=or_, device_id={"blk": peer},
        device_id_type=MESH)

    def ar_copy(step, n, to, source):
        i = groups[step][1]
        return pltpu.make_async_remote_copy(
            src_ref=arbuf.at[step, i], dst_ref=arbuf.at[step, i], send_sem=ars.at[step, n],
            recv_sem=arr.at[step, source], device_id=to, device_id_type=MESH)

    def ar_sends(step):
        size, i, mate = groups[step]
        sends = [ar_copy(step, j - 1, mate(j), i) for j in range(1, size)]
        if step == 2:
            sends += [ar_copy(step, size - 1 + j, z_odd(j), i) for j in range(size)]
        return sends

    def ar_send(step, value):
        arbuf[step, groups[step][1]] = value
        for c in ar_sends(step):
            c.start()

    def ar_sum(step, first=1):
        size, i, mate = groups[step]
        for j in range(first, size):
            ar_copy(step, 0, mate(j) if j else z_odd(0), lax.rem(i + j, size)).wait_recv()
        total = arbuf[step, 0]
        for j in range(1, size):
            total = total + arbuf[step, j]
        return total

    def before_first_near():
        @pl.when(even)
        def _():
            pl.semaphore_wait(bar, 6 + ZS + sum(size - 1 for size, _, _ in groups))
            for step in (1, -1, 3, -3):
                pl.semaphore_signal(rdy, inc=1, device_id={"blk": at(step)}, device_id_type=MESH)

        @pl.when(odd)
        def _():
            pl.semaphore_wait(rdy, 4)

        for j in range(ROWS // LB):
            peer_send(j).start()
        for r in (1, 2, 3):
            lab_send(r).start()
        for j in range(ROWS // LB):
            peer_send(j).wait_recv()
        lab_send(1).wait_recv()

    def both_z(k):
        z_send(0, k).start()
        z_send(1, k).start()

    def both_sent(k):
        z_send(0, k).wait_send()
        z_send(1, k).wait_send()

    def pump(k):
        z_send(F, k).wait_recv()
        fwd_f(k).start()
        z_send(N, k).wait_recv()
        fwd_n(k).start()

    def tell_peer(sem):
        pl.semaphore_signal(sem, inc=1, device_id={"blk": peer}, device_id_type=MESH)

    def before_3():
        @pl.when(odd)
        def _():
            each(0, GO_AT, both_sent)
            tell_peer(go)
            each(0, NCH, pump)

        @pl.when(even)
        def _():
            pl.semaphore_wait(go, 1)
            each(0, NCH, both_z)
            each(0, NCH, lambda k: fwd_f(k).wait_recv())

        for r in (2, 3):
            lab_send(r).wait_recv()

    def before_4():
        @pl.when(odd)
        def _():
            arbuf[3, 1] = tile()
            up.start()

        @pl.when(even)
        def _():
            each(0, NCH, lambda k: fwd_n(k).wait_recv())

    def before_5():
        @pl.when(odd)
        def _():
            pl.semaphore_wait(fargo, 1)
            each(0, NCH, lambda k: far_send(k).start())
            each(0, NCH, lambda k: fwd_f(k).wait_recv())

        @pl.when(even)
        def _():
            def quarter(t):
                q, own = t // 2, lax.rem(t, 2)

                @pl.when(own == 0)
                def _():
                    pump(2 * q)
                    pump(2 * q + 1)

                    @pl.when(q == 1)
                    def _():
                        each(0, GO_AT, both_sent)
                        tell_peer(fargo)

                c0 = pl.multiple_of(q * 128, 128)
                for rb in range(0, ROWS, 256):
                    sbuf[rb:rb + 256, :128] = scores(1, own, rb, 256, 2, c0, 128)
                tally(1, 2, c0, 128, (at(-own) - me) * ROWS)

                @pl.when(jnp.logical_and(own == 1, q >= 1))
                def _():
                    each(jnp.where(q == 1, 0, 2 * q), 2 * q + 2, lambda k: far_send(k).start())

            each(0, 8, quarter)
            up.wait_recv()
            ar_send(0, tile() + arbuf[3, 0])

    def before_6():
        @pl.when(odd)
        def _():
            each(0, NCH, lambda k: fwd_n(k).wait_recv())

    syncs = {2: before_first_near, 3: before_3, 4: before_4, 5: before_5, 6: before_6}

    def pair(i):
        for at_i, sync in syncs.items():
            pl.when(i == at_i)(sync)
        via_peer = jnp.logical_or(jnp.logical_and(i < 5, even), jnp.logical_and(i >= 5, odd))
        second = lax.rem(i, 2) == 0
        late_f = jnp.where(jnp.logical_xor(via_peer, second), F, N)
        f = jnp.where(i == 1, F, jnp.where(i < 3, N, late_f))
        r = jnp.where(i < 2, 0, jnp.where(i == 2, 1, jnp.where(via_peer, jnp.where(second, 3, 1), 2)))
        item(f, r, 0, ROWS, True)
        counted = jnp.where(even, jnp.where(f == 0, r <= 1, r == 3), jnp.logical_and(f == 0, r <= 2))

        @pl.when(counted)
        def _():
            tally(f, r, 0, ROWS)

    each(0, 7, pair)

    def finish(f, out):
        FB = 64

        def rows_(i):
            s = pl.ds(pl.multiple_of(i * FB, FB), FB)
            d = acc[f, s, :]
            r = rinv[f, s, 0:1]
            unit = raw[f, s, :].astype(F32) * r
            dot = jnp.sum(unit * d, axis=-1, keepdims=True)
            out[0, s, :] = ((d - unit * dot) * r).astype(BF16)

        each(0, ROWS // FB, rows_)

    def finish_flow(f):
        @pl.when(f == 0)
        def _():
            finish(0, o_img)

        @pl.when(f == 1)
        def _():
            finish(1, o_txt)

    @pl.when(even)
    def _():
        ar_send(1, ar_sum(0))

    each(0, 4, lambda k: far_recv(k).wait_recv())
    item(F, 3, 0, 256)
    finish_flow(N)

    def last(q):
        @pl.when(jnp.logical_and(even, q == 2))
        def _():
            ar_send(2, ar_sum(1))

        for j in (0, 1):
            far_recv(2 * q + j).wait_recv()
        item(F, 3, pl.multiple_of(q * 128, 128), 128)

    each(2, 4, last)
    finish_flow(F)

    @pl.when(odd)
    def _():
        ar_sum(2, 0)

    @pl.when(even)
    def _():
        ar_sum(2)

    fin = arbuf[2, 0]
    for j in range(1, ZS):
        fin = fin + arbuf[2, j]
    for i in range(3):
        o_stats[i] = jnp.sum(fin[i:i + 1, :]) / F32(blocks * reps * ROWS)

    each(GO_AT, NCH, both_sent)

    def left(k):
        fwd_f(k).wait_send()
        fwd_n(k).wait_send()
        far_send(k).wait_send()

    each(0, NCH, left)
    for j in range(ROWS // LB):
        peer_send(j).wait_send()
    for r in (1, 2, 3):
        lab_send(r).wait_send()

    @pl.when(odd)
    def _():
        up.wait_send()

    @pl.when(even)
    def _():
        for step in range(3):
            for c in ar_sends(step):
                c.wait_send()


def write_out(a, b, out_a, out_b, sems):
    copies = [pltpu.make_async_copy(v, o, sems.at[i]) for i, (v, o) in enumerate(((a, out_a), (b, out_b)))]
    for copy in copies:
        copy.start()
    for copy in copies:
        copy.wait()


def solution(mesh):
    blocks, reps = mesh.shape["blk"], mesh.shape["rep"]
    hbm = pl.BlockSpec(memory_space=pltpu.HBM)
    vmem = pl.BlockSpec(memory_space=pltpu.VMEM)
    smem = pl.BlockSpec(memory_space=pltpu.SMEM)
    dma = pltpu.SemaphoreType.DMA
    reg = pltpu.SemaphoreType.REGULAR

    def step(images, texts, labels, log_temp, bias):
        shape = (1, ROWS, D)
        *grads, stats = pl.pallas_call(
            functools.partial(kernel, blocks, reps),
            out_shape=(pltpu.VMEM(shape, BF16), pltpu.VMEM(shape, BF16), jax.ShapeDtypeStruct((3,), F32)),
            in_specs=[hbm, hbm, hbm, smem, smem],
            out_specs=(vmem, vmem, smem),
            scratch_shapes=[
                pltpu.VMEM((2, 4, ROWS, D), BF16),
                pltpu.VMEM((2, ROWS, D), BF16),
                pltpu.VMEM((2, ROWS, D), F32),
                pltpu.VMEM((2, ROWS, 128), F32),
                pltpu.VMEM((2, 4, 1, ROWS), jnp.int32),
                pltpu.VMEM((2, ROWS, 128), jnp.int32),
                pltpu.VMEM((2, 1, ROWS), F32),
                pltpu.VMEM((ROWS, ROWS), F32),
                pltpu.VMEM((3, 8, 128), F32),
                pltpu.VMEM((4, 8, 8, 128), F32),
                dma((2, 4)), dma,
                dma((2, NCH)), dma((2, NCH)), dma((4,)), dma((4,)),
                dma((NCH,)), dma((NCH,)), dma((NCH,)), dma((NCH,)), dma((NCH,)), dma((NCH,)),
                dma((3,)), dma((3,)),
                dma, dma, dma((3, 16)), dma((3, 8)),
                reg, reg, reg,
            ],
            compiler_params=pltpu.CompilerParams(
                collective_id=0, has_side_effects=True, vmem_limit_bytes=48 * 2**20),
            name="siglip",
        )(*[pltpu.with_memory_space_constraint(v, pltpu.HBM) for v in (images, texts, labels)], log_temp, bias)

        full = jax.ShapeDtypeStruct(shape, BF16)
        anywhere = pl.BlockSpec(memory_space=pl.ANY)
        written = pl.pallas_call(
            write_out,
            out_shape=(full, full),
            in_specs=[anywhere] * 2,
            out_specs=(hbm, hbm),
            scratch_shapes=[dma((2,))],
            name="write_out",
        )(*[pltpu.with_memory_space_constraint(v, pltpu.VMEM) for v in grads])
        return *written, stats

    return jax.shard_map(
        step,
        mesh=mesh,
        in_specs=(P("rep", "blk", None), P("rep", "blk", None), P("rep", "blk"), P(), P()),
        out_specs=(P("rep", "blk", None), P("rep", "blk", None), P()),
        check_vma=False,
    )
```
